32 devices in a mesh: grp: 2 (over x), gx: 16 (over z, y, core).
Axes of the slice: x: 2, y: 2, z: 4, core: 2. Of those that a mesh axis runs over, the one named last changes fastest.
Arguments:
- permeability: float32 [256, 64, 128], P('gx', 'grp'), parts along dimension 1, may hold values from 0.1 to 10
- sources: float32 [8, 256, 64, 128], P(None, 'gx', 'grp'), parts along dimension 2, may hold values from -1 to 2
Outputs:
- block_stiffness: float32 [8, 8, 16, 4, 8], P(None, None, 'gx', 'grp'), parts along dimension 3
- face_stiffness: float32 [3, 8, 8, 16, 4, 8], P(None, None, None, 'gx', 'grp'), parts along dimension 4
The draws below stay inside these ranges and needn't reach their ends.
There are 2 independent parts, one for each index of `grp`. The reference program is written for one: setup_inputs(seed, part) draws one part's arguments, and reference() takes and returns one part's arrays. A program takes and returns all parts, laid end to end along the dimension named above; each array names one. Nothing has to cross between parts.
All inputs are finite; a program needn't handle non-finite values.
Results may differ from the reference program's by a relative error of at most 0.0049.
Values sent between devices are 32-bit elements; how exact they have to be, the bound alone decides.
A program may use at most 256 MiB of HBM per device.

```python
import math
import jax
import jax.numpy as jnp
from jax import lax

B = 16
BASIS = 8
SWEEPS = 4
NX = 256
NY = 32
NZ = 128


def block_levels(own_key, shape, shards, smallest, top_value):
    level, own = 1.0, jax.random.fold_in(own_key, 6)
    for dim, blocks in shards:
        steps = jnp.exp(jax.random.uniform(jax.random.fold_in(own, dim), (blocks,), jnp.float32, smallest / len(shards), top_value / len(shards)))
        level = level * jnp.repeat(steps, shape[dim] // blocks).reshape([-1 if axis == dim else 1 for axis in range(len(shape))])
    return level


def setup_inputs(seed: int = 0, part: int = 0) -> dict:
    keys = jax.random.split(jax.random.key(seed), 3)
    part_keys = jax.random.split(jax.random.fold_in(keys[2], part), 3)
    permeability = jnp.clip(jnp.exp(math.log(10.0) - 4.6051702 * jax.random.uniform(part_keys[0], (NX, NY, NZ), jnp.float32) ** block_levels(part_keys[0], (NX, NY, NZ), ((0, 16),), -0.2, 0.2)), 0.1, 10.0)
    sources = jnp.clip(-1.0 + 3.0 * jax.random.uniform(part_keys[1], (BASIS, NX, NY, NZ), jnp.float32) ** block_levels(part_keys[1], (BASIS, NX, NY, NZ), ((1, 16),), -0.2, 0.2), -1.0, 2.0)
    return dict(permeability=permeability, sources=sources)


WEIGHT_Z = 0.1


def conduct(perm_field):
    padded = jnp.pad(perm_field, 1)
    face_x = 0.5 * (padded[1:, 1:-1, 1:-1] + padded[:-1, 1:-1, 1:-1])
    face_y = 0.5 * (padded[1:-1, 1:, 1:-1] + padded[1:-1, :-1, 1:-1])
    face_z = (0.5 * WEIGHT_Z) * (padded[1:-1, 1:-1, 1:] + padded[1:-1, 1:-1, :-1])
    diagonal = face_x[:-1] + face_x[1:] + face_y[:, :-1] + face_y[:, 1:] + face_z[:, :, :-1] + face_z[:, :, 1:]
    return face_x, face_y, face_z, diagonal


def neighbors(basis, face_x, face_y, face_z):
    padded = jnp.pad(basis, ((0, 0), (1, 1), (1, 1), (1, 1)))
    total = face_x[1:] * padded[:, 2:, 1:-1, 1:-1] + face_x[:-1] * padded[:, :-2, 1:-1, 1:-1]
    total = total + face_y[:, 1:] * padded[:, 1:-1, 2:, 1:-1] + face_y[:, :-1] * padded[:, 1:-1, :-2, 1:-1]
    total = total + face_z[:, :, 1:] * padded[:, 1:-1, 1:-1, 2:] + face_z[:, :, :-1] * padded[:, 1:-1, 1:-1, :-2]
    return total


def couple(basis, face_x, face_y, face_z, diagonal, beyond):
    length_x, length_y, length_z = basis.shape[1], basis.shape[2], basis.shape[3]
    shape_blocks = (length_x // B, B, length_y // B, B, length_z)

    def tiles(values):
        return values.reshape(values.shape[:-3] + shape_blocks)

    def contract(left, right):
        lines = jnp.einsum('cixjyz,eixjyz->ceijz', left, right, precision=lax.Precision.HIGHEST)
        return jnp.sum(lines.reshape(lines.shape[:-1] + (length_z // B, B)), axis=-1)

    place_z = jnp.arange(length_z, dtype=jnp.int32) % B
    last_z = (place_z == B - 1).astype(basis.dtype)
    inner_mask = 1.0 - last_z
    tiled = tiles(basis)
    self_terms = contract(tiled * tiles(diagonal), tiled)
    upper_x = tiles(jnp.concatenate([basis[:, 1:], beyond[:, None]], axis=1))
    upper_y = tiles(jnp.pad(basis[:, :, 1:], ((0, 0), (0, 0), (0, 1), (0, 0))))
    upper_z = tiles(jnp.pad(basis[:, :, :, 1:], ((0, 0), (0, 0), (0, 0), (0, 1))))
    weight_x = tiles(face_x[1:]) * tiled
    weight_y = tiles(face_y[:, 1:]) * tiled
    weight_z = tiles(face_z[:, :, 1:]) * tiled
    inner_x = contract(weight_x[:, :, :B - 1], upper_x[:, :, :B - 1])
    cross_x = contract(weight_x[:, :, B - 1:], upper_x[:, :, B - 1:])
    inner_y = contract(weight_y[:, :, :, :, :B - 1], upper_y[:, :, :, :, :B - 1])
    cross_y = contract(weight_y[:, :, :, :, B - 1:], upper_y[:, :, :, :, B - 1:])
    inner_z = contract(weight_z * inner_mask, upper_z)
    cross_z = contract(weight_z * last_z, upper_z)
    inner_sum = inner_x + inner_y + inner_z
    block_part = self_terms - inner_sum - jnp.transpose(inner_sum, (1, 0, 2, 3, 4))
    face_part = -jnp.stack([cross_x, cross_y, cross_z])
    return block_part / (B ** 3), face_part / (B ** 2)


def reference(permeability, sources):
    face_x, face_y, face_z, diagonal = conduct(permeability)
    basis = sources / diagonal
    for repeat in range(SWEEPS - 1):
        basis = (sources + neighbors(basis, face_x, face_y, face_z)) / diagonal
    beyond = jnp.zeros((sources.shape[0], sources.shape[2], sources.shape[3]), sources.dtype)
    return couple(basis, face_x, face_y, face_z, diagonal, beyond)
```

```python
import functools

import jax
import jax.numpy as jnp
from jax import lax
from jax.experimental import pallas as pl
from jax.experimental.pallas import tpu as pltpu
from jax.sharding import PartitionSpec as P

B = 16
WEIGHT_Z = 0.1
NF = 8
NXL = 16
NY = 32
NZ = 128
LO = 3
HI = 4
LAYERS = LO + NXL + HI
ROWS = 8 + NF * NY + 8
NU = 9
F32 = jnp.float32
HIGH = lax.Precision.HIGHEST
MESH = pl.DeviceIdType.MESH


def kernel(n, perm, src, blk_out, face_out,
           K, S, B0, B1, B2, B3, W, U, WX, ACC, CX, CY, VV, VW, RED,
           load_sem, send_sem, recv_sem):
    me = lax.axis_index("gx")
    has_low = me > 0
    has_high = me < n - 1

    barrier = pltpu.get_barrier_semaphore()

    @pl.when(has_low)
    def _():
        pl.semaphore_signal(barrier, inc=1, device_id={"gx": me - 1}, device_id_type=MESH)

    @pl.when(has_high)
    def _():
        pl.semaphore_signal(barrier, inc=1, device_id={"gx": me + 1}, device_id_type=MESH)

    loads = [pltpu.make_async_copy(perm, K.at[pl.ds(LO + 1, NXL), pl.ds(8, NY)], load_sem.at[NF])]
    for c in range(NF):
        loads.append(pltpu.make_async_copy(
            src.at[c], S.at[pl.ds(LO, NXL), pl.ds(c * NY, NY)], load_sem.at[c]))
    for copy in loads:
        copy.start()

    zero8 = jnp.zeros((8, NZ), F32)

    def pads(l, carry):
        K[l, pl.ds(0, 8), :] = zero8
        K[l, pl.ds(8 + NY, 8), :] = zero8
        return carry

    lax.fori_loop(0, LAYERS + 2, pads, 0)

    def pads_b(l, carry):
        base = pl.multiple_of(l * ROWS, 8)
        for ref in (B0, B1, B2, B3):
            ref[pl.ds(base, 8), :] = zero8
            ref[pl.ds(base + ROWS - 8, 8), :] = zero8
        return carry

    lax.fori_loop(0, LAYERS, pads_b, 0)
    for l in (LO - 1, LO + NXL):
        B3[pl.ds(l * ROWS, ROWS), :] = jnp.zeros((ROWS, NZ), F32)
    ACC[...] = jnp.zeros_like(ACC)

    @pl.when(me == 0)
    def _():
        K[pl.ds(0, LO + 1), pl.ds(8, NY), :] = jnp.zeros((LO + 1, NY, NZ), F32)

        def clear(l, carry):
            S[l] = jnp.zeros((NF * NY, NZ), F32)
            return carry

        lax.fori_loop(0, LO, clear, 0)

    @pl.when(me == n - 1)
    def _():
        K[pl.ds(LO + NXL + 1, HI + 1), pl.ds(8, NY), :] = jnp.zeros((HI + 1, NY, NZ), F32)

        def clear(l, carry):
            S[l] = jnp.zeros((NF * NY, NZ), F32)
            return carry

        lax.fori_loop(LO + NXL, LAYERS, clear, 0)

    def up_perm():
        return pltpu.make_async_remote_copy(
            src_ref=K.at[pl.ds(NXL, LO + 1), pl.ds(8, NY)],
            dst_ref=K.at[pl.ds(0, LO + 1), pl.ds(8, NY)],
            send_sem=send_sem.at[0, 0], recv_sem=recv_sem.at[0, 0],
            device_id={"gx": me + 1}, device_id_type=MESH)

    def down_perm():
        return pltpu.make_async_remote_copy(
            src_ref=K.at[pl.ds(LO + 1, HI + 1), pl.ds(8, NY)],
            dst_ref=K.at[pl.ds(LO + NXL + 1, HI + 1), pl.ds(8, NY)],
            send_sem=send_sem.at[1, 0], recv_sem=recv_sem.at[1, 0],
            device_id={"gx": me - 1}, device_id_type=MESH)

    def up_layer(k):
        return pltpu.make_async_remote_copy(
            src_ref=S.at[LO + NXL - k], dst_ref=S.at[LO - k],
            send_sem=send_sem.at[0, k], recv_sem=recv_sem.at[0, k],
            device_id={"gx": me + 1}, device_id_type=MESH)

    def down_layer(k):
        return pltpu.make_async_remote_copy(
            src_ref=S.at[LO - 1 + k], dst_ref=S.at[LO + NXL - 1 + k],
            send_sem=send_sem.at[1, k], recv_sem=recv_sem.at[1, k],
            device_id={"gx": me - 1}, device_id_type=MESH)

    pl.semaphore_wait(barrier, has_low.astype(jnp.int32) + has_high.astype(jnp.int32))

    loads[0].wait()

    @pl.when(has_low)
    def _():
        down_perm().start()

    @pl.when(has_high)
    def _():
        up_perm().start()

    for copy in loads[1:]:
        copy.wait()

    @pl.when(has_low)
    def _():
        for k in range(1, HI + 1):
            down_layer(k).start()

    @pl.when(has_high)
    def _():
        for k in range(1, LO + 1):
            up_layer(k).start()

    lane = lax.broadcasted_iota(jnp.int32, (8, NZ), 1)
    sub = lax.broadcasted_iota(jnp.int32, (8, NZ), 0)
    low_lane = lane == 0
    high_lane = lane == NZ - 1
    place = lane % B
    block_first = place == 0
    block_last = place == B - 1

    def prep(l, own):
        dead = jnp.logical_or(jnp.logical_and(l < LO, me == 0),
                              jnp.logical_and(l >= LO + NXL, me == n - 1))
        alive = jnp.where(dead, 0.0, 1.0).astype(F32)
        x = l - LO
        for t in range(4):
            k = K[l + 1, pl.ds(8 + 8 * t, 8), :]
            fxm = 0.5 * (k + K[l, pl.ds(8 + 8 * t, 8), :])
            fxp = 0.5 * (k + K[l + 2, pl.ds(8 + 8 * t, 8), :])
            fym = 0.5 * (k + K[l + 1, pl.ds(7 + 8 * t, 8), :])
            fyp = 0.5 * (k + K[l + 1, pl.ds(9 + 8 * t, 8), :])
            fzm = (0.5 * WEIGHT_Z) * (k + jnp.where(low_lane, 0.0, pltpu.roll(k, 1, 1)))
            fzp = (0.5 * WEIGHT_Z) * (k + jnp.where(high_lane, 0.0, pltpu.roll(k, NZ - 1, 1)))
            d = fxm + fxp + fym + fyp + fzm + fzp
            inv = jnp.where(alive > 0.5, 1.0 / d, 0.0)
            if t == 0:
                fym = jnp.where(sub == 0, 0.0, fym)
            if t == 3:
                fyp = jnp.where(sub == 7, 0.0, fyp)
            fzm = jnp.where(low_lane, 0.0, fzm)
            fzp = jnp.where(high_lane, 0.0, fzp)
            for q, f in enumerate((fxm, fxp, fym, fyp, fzm, fzp)):
                W[l, q, pl.ds(8 * t, 8), :] = f * inv
            W[l, 6, pl.ds(8 * t, 8), :] = inv
            if own:
                inner_m = jnp.where(x == 0, 0.0, 1.0).astype(F32)
                inner_p = jnp.where(x == NXL - 1, 0.0, 1.0).astype(F32)
                base = pl.multiple_of(x * (NU * NY), 8) + 8 * t

                def put(q, f):
                    U[pl.ds(base + q * NY, 8), :] = f

                put(0, fxm * inner_m)
                put(1, fxp * inner_p)
                put(2, jnp.where(sub == 0, 0.0, fym) if t == 2 else fym)
                put(3, jnp.where(sub == 7, 0.0, fyp) if t == 1 else fyp)
                put(4, jnp.where(block_first, 0.0, fzm))
                put(5, jnp.where(block_last, 0.0, fzp))
                put(6, d)
                spread = jnp.where(block_last, fzp, pltpu.roll(fzp, 1, 1))
                near = jnp.logical_or(block_last, block_first)
                spread = jnp.where(near, spread, pltpu.roll(spread, 2, 1))
                near = jnp.logical_or(block_last, place <= 2)
                spread = jnp.where(near, spread, pltpu.roll(spread, 4, 1))
                near = jnp.logical_or(block_last, place <= 6)
                spread = jnp.where(near, spread, pltpu.roll(spread, 8, 1))
                put(7, spread)
                put(8, fyp)

                @pl.when(x == NXL - 1)
                def _():
                    WX[pl.ds(8 * t, 8), :] = fxp

    def first(l):
        base = pl.multiple_of(l * ROWS, 8) + 8
        for t in range(4):
            inv = W[l, 6, pl.ds(8 * t, 8), :]
            for c in range(NF):
                r = c * NY + 8 * t
                B0[pl.ds(base + r, 8), :] = S[l, pl.ds(r, 8), :] * inv

    def sweep(old, new, l):
        base = pl.multiple_of(l * ROWS, 8) + 8
        for t in range(4):
            wxm, wxp, wym, wyp, wzm, wzp = [W[l, q, pl.ds(8 * t, 8), :] for q in range(6)]
            for c in range(NF):
                r = base + c * NY + 8 * t
                mid = old[pl.ds(r, 8), :]
                x_part = wxm * old[pl.ds(r - ROWS, 8), :] + wxp * old[pl.ds(r + ROWS, 8), :]
                y_part = wym * old[pl.ds(r - 1, 8), :] + wyp * old[pl.ds(r + 1, 8), :]
                z_part = wzm * pltpu.roll(mid, 1, 1) + wzp * pltpu.roll(mid, NZ - 1, 1)
                new[pl.ds(r, 8), :] = (B0[pl.ds(r, 8), :] + x_part) + (y_part + z_part)

    def many(body, start, step, count):
        def run(i, carry):
            body(start + i * step)
            return carry

        lax.fori_loop(0, count, run, 0)

    pairs = [(c, e) for c in range(NF) for e in range(c, NF)]
    near1 = jnp.logical_or(block_last, block_first)
    near2 = jnp.logical_or(block_last, place <= 2)
    near3 = jnp.logical_or(block_last, place <= 6)

    def couple(start, step, count):
        for yb in range(2):
            def run(i, accs):
                l = start + i * step
                x = l - LO
                base = pl.multiple_of(l * ROWS, 8) + 8
                ubase = pl.multiple_of(x * (NU * NY), 8)
                accs = list(accs)
                for tt in range(2):
                    t = 2 * yb + tt
                    u = [U[pl.ds(ubase + q * NY + 8 * t, 8), :] for q in range(7)]
                    bs = [B3[pl.ds(base + c * NY + 8 * t, 8), :] for c in range(NF)]
                    for e in range(NF):
                        r = base + e * NY + 8 * t
                        total = u[6] * bs[e]
                        total -= u[0] * B3[pl.ds(r - ROWS, 8), :] + u[1] * B3[pl.ds(r + ROWS, 8), :]
                        total -= u[2] * B3[pl.ds(r - 1, 8), :] + u[3] * B3[pl.ds(r + 1, 8), :]
                        total -= u[4] * pltpu.roll(bs[e], 1, 1) + u[5] * pltpu.roll(bs[e], NZ - 1, 1)
                        for p, (c, e2) in enumerate(pairs):
                            if e2 == e:
                                accs[p] = accs[p] + bs[c] * total
                    m = [jnp.where(near1, bs[2 * q], pltpu.roll(bs[2 * q + 1], 2, 1)) for q in range(4)]
                    m = [jnp.where(near2, m[2 * q], pltpu.roll(m[2 * q + 1], 4, 1)) for q in range(2)]
                    v = jnp.where(near3, m[0], pltpu.roll(m[1], 8, 1))
                    vr = pl.ds(pl.multiple_of(yb * 256 + x * 16, 8) + 8 * tt, 8)
                    VV[vr, :] = v
                    VW[vr, :] = v * U[pl.ds(ubase + 7 * NY + 8 * t, 8), :]
                return tuple(accs)

            accs = tuple(ACC[yb, p] for p in range(len(pairs)))
            accs = lax.fori_loop(0, count, run, accs)
            for p in range(len(pairs)):
                ACC[yb, p] = accs[p]

    def prep_first(l):
        prep(l, True)
        first(l)

    many(prep_first, LO + 1, 1, NXL - 2)
    many(functools.partial(sweep, B0, B1), LO + 2, 1, NXL - 4)
    many(functools.partial(sweep, B1, B2), LO + 3, 1, NXL - 6)
    many(functools.partial(sweep, B2, B3), LO + 4, 1, NXL - 8)
    couple(LO + 5, 1, NXL - 10)

    @pl.when(has_low)
    def _():
        up_perm().wait_recv()

    @pl.when(has_high)
    def _():
        down_perm().wait_recv()

    many(prep_first, LO, NXL - 1, 2)
    many(lambda l: prep(l, False), 0, 1, LO)
    many(lambda l: prep(l, False), LO + NXL, 1, HI)

    def stage(k, carry):
        @pl.when(jnp.logical_and(has_low, k > 0))
        def _():
            up_layer(k).wait_recv()

        @pl.when(jnp.logical_and(has_high, k > 0))
        def _():
            down_layer(k).wait_recv()

        @pl.when(k > 0)
        def _():
            many(first, LO - k, NXL - 1 + 2 * k, 2)

        many(functools.partial(sweep, B0, B1), LO + 1 - k, NXL - 3 + 2 * k, 2)
        many(functools.partial(sweep, B1, B2), LO + 2 - k, NXL - 5 + 2 * k, 2)
        many(functools.partial(sweep, B2, B3), LO + 3 - k, NXL - 7 + 2 * k, 2)
        couple(LO + 4 - k, NXL - 9 + 2 * k, 2)
        return carry

    lax.fori_loop(0, LO + 1, stage, 0)
    couple(LO, NXL - 1, 2)

    for h in range(2):
        def rows(ref, first_row, stride):
            return ref[pl.ds(first_row, 8, stride=stride), :]

        wy = rows(U, (8 * h * NU + 8) * NY + B - 1, NU * NY)
        left = [wy * rows(B3, (LO + 8 * h) * ROWS + 8 + c * NY + B - 1, ROWS) for c in range(NF)]
        right = [rows(B3, (LO + 8 * h) * ROWS + 8 + e * NY + B, ROWS) for e in range(NF)]
        for c in range(NF):
            for e in range(NF):
                value = left[c] * right[e]
                if h == 0:
                    CY[pl.ds((c * NF + e) * 8, 8), :] = value
                else:
                    CY[pl.ds((c * NF + e) * 8, 8), :] += value

    @pl.when(has_high)
    def _():
        down_layer(HI).wait_recv()

    first(LO + NXL + 3)
    sweep(B0, B1, LO + NXL + 2)
    sweep(B1, B2, LO + NXL + 1)
    sweep(B2, B3, LO + NXL)

    base = (LO + NXL - 1) * ROWS + 8
    for yb in range(2):
        def pick(layer, c, tt):
            return B3[pl.ds(base + layer * ROWS + c * NY + 16 * yb + 8 * tt, 8), :]

        right = [[pick(1, e, tt) for e in range(NF)] for tt in range(2)]
        wx = [WX[pl.ds(16 * yb + 8 * tt, 8), :] for tt in range(2)]
        for c in range(NF):
            left = [wx[tt] * pick(0, c, tt) for tt in range(2)]
            for e in range(NF):
                CX[pl.ds(((c * NF + e) * 2 + yb) * 8, 8), :] = left[0] * right[0][e] + left[1] * right[1][e]

    def fold(ref, first_row):
        total = ref[pl.ds(first_row, 8, stride=8), :]
        for s in range(1, 8):
            total = total + ref[pl.ds(first_row + s, 8, stride=8), :]
        return total

    zi = lax.broadcasted_iota(jnp.int32, (NZ, NZ), 0)
    zj = lax.broadcasted_iota(jnp.int32, (NZ, NZ), 1)
    group = (zi // B == zj).astype(F32)

    for yb in range(2):
        for p, (c, e) in enumerate(pairs):
            value = ACC[yb, p]
            RED[pl.ds(((c * NF + e) * 2 + yb) * 8, 8), :] = value
            if c != e:
                RED[pl.ds(((e * NF + c) * 2 + yb) * 8, 8), :] = value

    def dot(a, b):
        return lax.dot_general(a, b, (((1,), (0,)), ((), ())), precision=HIGH, preferred_element_type=F32)

    blk = jnp.concatenate([fold(RED, 64 * q) for q in range(16)], axis=0)
    blk_out[...] = dot(blk, group)[:, :8] * (1.0 / B**3)
    fx = jnp.concatenate([fold(CX, 64 * q) for q in range(16)], axis=0)
    face_out[pl.ds(0, 128), :] = dot(fx, group)[:, :8] * (-1.0 / B**2)

    fy = jnp.concatenate([fold(CY, 64 * q) for q in range(8)], axis=0)
    fy = dot(fy, group) * (-1.0 / B**2)
    zeros64 = jnp.zeros((64, NZ), F32)
    RED[pl.ds(0, 64, stride=2), :] = fy
    RED[pl.ds(1, 64, stride=2), :] = zeros64

    def slot(z):
        s = lax.rem(z - (B - 1) + NZ, NZ)
        return s // B, (s % B) // 2, s % 2

    ij, ic, ip = slot(zi)
    jj, je, jp = slot(zj)
    keep = jnp.logical_and(jnp.logical_and(ij == jj, ij < NZ // B - 1), jnp.logical_and(ip == 0, jp == 1))
    spread = jnp.logical_and(ip == 1, zj == ic * 8 + ij).astype(F32)
    wide = lax.broadcasted_iota(jnp.int32, (8, NZ), 1)
    wj, wc, wp = slot(wide)
    gather = jnp.logical_and(wp == 0, wc == lax.broadcasted_iota(jnp.int32, (8, NZ), 0)).astype(F32)
    for yb in range(2):
        gram = lax.dot_general(VV[pl.ds(yb * 256, 256), :], VW[pl.ds(yb * 256, 256), :],
                               (((0,), (0,)), ((), ())), precision=HIGH, preferred_element_type=F32)
        gram = jnp.where(keep, gram, 0.0)
        out = dot(gather, dot(gram, spread)) * (-1.0 / B**2)
        for e in range(NF):
            value = out if e == 0 else pltpu.roll(out, NZ - 8 * e, 1)
            RED[pl.ds(128 + e * 2 + yb, 8, stride=16), :] = value
    face_out[pl.ds(128, 256), :] = RED[pl.ds(0, 256), :][:, :8]

    @pl.when(has_low)
    def _():
        down_perm().wait_send()
        for k in range(1, HI + 1):
            down_layer(k).wait_send()

    @pl.when(has_high)
    def _():
        up_perm().wait_send()
        for k in range(1, LO + 1):
            up_layer(k).wait_send()


def on_device(n, permeability, sources):
    blk, face = pl.pallas_call(
        functools.partial(kernel, n),
        out_shape=(jax.ShapeDtypeStruct((NF * NF * 2, 8), F32),
                   jax.ShapeDtypeStruct((3 * NF * NF * 2, 8), F32)),
        in_specs=[pl.BlockSpec(memory_space=pl.ANY)] * 2,
        out_specs=(pl.BlockSpec(memory_space=pltpu.VMEM),) * 2,
        scratch_shapes=[
            pltpu.VMEM((LAYERS + 2, NY + 16, NZ), F32),
            pltpu.VMEM((LAYERS, NF * NY, NZ), F32),
            pltpu.VMEM((LAYERS * ROWS, NZ), F32),
            pltpu.VMEM((LAYERS * ROWS, NZ), F32),
            pltpu.VMEM((LAYERS * ROWS, NZ), F32),
            pltpu.VMEM((LAYERS * ROWS, NZ), F32),
            pltpu.VMEM((LAYERS, 7, NY, NZ), F32),
            pltpu.VMEM((NXL * NU * NY, NZ), F32),
            pltpu.VMEM((NY, NZ), F32),
            pltpu.VMEM((2, 36, 8, NZ), F32),
            pltpu.VMEM((NF * NF * 2 * 8, NZ), F32),
            pltpu.VMEM((NF * NF * 8, NZ), F32),
            pltpu.VMEM((512, NZ), F32),
            pltpu.VMEM((512, NZ), F32),
            pltpu.VMEM((NF * NF * 2 * 8, NZ), F32),
            pltpu.SemaphoreType.DMA((NF + 1,)),
            pltpu.SemaphoreType.DMA((2, HI + 1)),
            pltpu.SemaphoreType.DMA((2, HI + 1)),
        ],
        compiler_params=pltpu.CompilerParams(
            collective_id=0, has_side_effects=True, vmem_limit_bytes=40 * 1024 * 1024),
    )(permeability, sources)
    return blk.reshape(NF, NF, 1, 2, 8), face.reshape(3, NF, NF, 1, 2, 8)


def solution(mesh):
    return jax.shard_map(
        functools.partial(on_device, mesh.shape["gx"]),
        mesh=mesh,
        in_specs=(P("gx", "grp", None), P(None, "gx", "grp", None)),
        out_specs=(P(None, None, "gx", "grp", None), P(None, None, None, "gx", "grp", None)),
        check_vma=False,
    )
```

```python
import functools

import jax
import jax.numpy as jnp
from jax import lax
from jax.experimental import pallas as pl
from jax.experimental.pallas import tpu as pltpu
from jax.sharding import PartitionSpec as P

B = 16
WEIGHT_Z = 0.1
NF = 8
NXL = 16
NY = 32
NZ = 128
LO = 3
HI = 4
LAYERS = LO + NXL + HI
ROWS = 8 + NF * NY + 8
NU = 9
F32 = jnp.float32
HIGH = lax.Precision.HIGHEST
MESH = pl.DeviceIdType.MESH


def kernel(n, perm, src, blk_out, face_out,
           K, S, B0, B1, B2, B3, W, U, WX, ACC, CX, CY, VV, VW, RED, TOT,
           load_sem, send_sem, recv_sem):
    me = lax.axis_index("gx")
    has_low = me > 0
    has_high = me < n - 1

    barrier = pltpu.get_barrier_semaphore()

    @pl.when(has_low)
    def _():
        pl.semaphore_signal(barrier, inc=1, device_id={"gx": me - 1}, device_id_type=MESH)

    @pl.when(has_high)
    def _():
        pl.semaphore_signal(barrier, inc=1, device_id={"gx": me + 1}, device_id_type=MESH)

    loads = [pltpu.make_async_copy(perm, K.at[pl.ds(LO + 1, NXL), pl.ds(8, NY)], load_sem.at[NF])]
    for c in range(NF):
        loads.append(pltpu.make_async_copy(
            src.at[c], S.at[pl.ds(LO, NXL), pl.ds(c * NY, NY)], load_sem.at[c]))
    for copy in loads:
        copy.start()

    zero8 = jnp.zeros((8, NZ), F32)

    def pads(l, carry):
        K[l, pl.ds(0, 8), :] = zero8
        K[l, pl.ds(8 + NY, 8), :] = zero8
        return carry

    lax.fori_loop(0, LAYERS + 2, pads, 0)

    def pads_b(l, carry):
        base = pl.multiple_of(l * ROWS, 8)
        for ref in (B0, B1, B2, B3):
            ref[pl.ds(base, 8), :] = zero8
            ref[pl.ds(base + ROWS - 8, 8), :] = zero8
        return carry

    lax.fori_loop(0, LAYERS, pads_b, 0)
    for l in (LO - 1, LO + NXL):
        B3[pl.ds(l * ROWS, ROWS), :] = jnp.zeros((ROWS, NZ), F32)
    ACC[...] = jnp.zeros_like(ACC)

    @pl.when(me == 0)
    def _():
        K[pl.ds(0, LO + 1), pl.ds(8, NY), :] = jnp.zeros((LO + 1, NY, NZ), F32)

        def clear(l, carry):
            S[l] = jnp.zeros((NF * NY, NZ), F32)
            return carry

        lax.fori_loop(0, LO, clear, 0)

    @pl.when(me == n - 1)
    def _():
        K[pl.ds(LO + NXL + 1, HI + 1), pl.ds(8, NY), :] = jnp.zeros((HI + 1, NY, NZ), F32)

        def clear(l, carry):
            S[l] = jnp.zeros((NF * NY, NZ), F32)
            return carry

        lax.fori_loop(LO + NXL, LAYERS, clear, 0)

    def up_perm():
        return pltpu.make_async_remote_copy(
            src_ref=K.at[pl.ds(NXL, LO + 1), pl.ds(8, NY)],
            dst_ref=K.at[pl.ds(0, LO + 1), pl.ds(8, NY)],
            send_sem=send_sem.at[0, 0], recv_sem=recv_sem.at[0, 0],
            device_id={"gx": me + 1}, device_id_type=MESH)

    def down_perm():
        return pltpu.make_async_remote_copy(
            src_ref=K.at[pl.ds(LO + 1, HI + 1), pl.ds(8, NY)],
            dst_ref=K.at[pl.ds(LO + NXL + 1, HI + 1), pl.ds(8, NY)],
            send_sem=send_sem.at[1, 0], recv_sem=recv_sem.at[1, 0],
            device_id={"gx": me - 1}, device_id_type=MESH)

    def up_layer(k):
        return pltpu.make_async_remote_copy(
            src_ref=S.at[LO + NXL - k], dst_ref=S.at[LO - k],
            send_sem=send_sem.at[0, k], recv_sem=recv_sem.at[0, k],
            device_id={"gx": me + 1}, device_id_type=MESH)

    def down_layer(k):
        return pltpu.make_async_remote_copy(
            src_ref=S.at[LO - 1 + k], dst_ref=S.at[LO + NXL - 1 + k],
            send_sem=send_sem.at[1, k], recv_sem=recv_sem.at[1, k],
            device_id={"gx": me - 1}, device_id_type=MESH)

    pl.semaphore_wait(barrier, has_low.astype(jnp.int32) + has_high.astype(jnp.int32))

    loads[0].wait()

    @pl.when(has_low)
    def _():
        down_perm().start()

    @pl.when(has_high)
    def _():
        up_perm().start()

    for copy in loads[1:]:
        copy.wait()

    @pl.when(has_low)
    def _():
        for k in range(1, HI + 1):
            down_layer(k).start()

    @pl.when(has_high)
    def _():
        for k in range(1, LO + 1):
            up_layer(k).start()

    lane = lax.broadcasted_iota(jnp.int32, (8, NZ), 1)
    sub = lax.broadcasted_iota(jnp.int32, (8, NZ), 0)
    low_lane = lane == 0
    high_lane = lane == NZ - 1
    place = lane % B
    block_first = place == 0
    block_last = place == B - 1

    def prep(l, own):
        dead = jnp.logical_or(jnp.logical_and(l < LO, me == 0),
                              jnp.logical_and(l >= LO + NXL, me == n - 1))
        alive = jnp.where(dead, 0.0, 1.0).astype(F32)
        x = l - LO
        for t in range(4):
            k = K[l + 1, pl.ds(8 + 8 * t, 8), :]
            fxm = 0.5 * (k + K[l, pl.ds(8 + 8 * t, 8), :])
            fxp = 0.5 * (k + K[l + 2, pl.ds(8 + 8 * t, 8), :])
            fym = 0.5 * (k + K[l + 1, pl.ds(7 + 8 * t, 8), :])
            fyp = 0.5 * (k + K[l + 1, pl.ds(9 + 8 * t, 8), :])
            fzm = (0.5 * WEIGHT_Z) * (k + jnp.where(low_lane, 0.0, pltpu.roll(k, 1, 1)))
            fzp = (0.5 * WEIGHT_Z) * (k + jnp.where(high_lane, 0.0, pltpu.roll(k, NZ - 1, 1)))
            d = fxm + fxp + fym + fyp + fzm + fzp
            inv = jnp.where(alive > 0.5, 1.0 / d, 0.0)
            if t == 0:
                fym = jnp.where(sub == 0, 0.0, fym)
            if t == 3:
                fyp = jnp.where(sub == 7, 0.0, fyp)
            fzm = jnp.where(low_lane, 0.0, fzm)
            fzp = jnp.where(high_lane, 0.0, fzp)
            for q, f in enumerate((fxm, fxp, fym, fyp, fzm, fzp)):
                W[l, q, pl.ds(8 * t, 8), :] = f * inv
            W[l, 6, pl.ds(8 * t, 8), :] = inv
            if own:
                inner_m = jnp.where(x == 0, 0.0, 1.0).astype(F32)
                inner_p = jnp.where(x == NXL - 1, 0.0, 1.0).astype(F32)
                base = pl.multiple_of(x * (NU * NY), 8) + 8 * t

                def put(q, f):
                    U[pl.ds(base + q * NY, 8), :] = f

                put(0, fxm * inner_m)
                put(1, fxp * inner_p)
                put(2, jnp.where(sub == 0, 0.0, fym) if t == 2 else fym)
                put(3, jnp.where(sub == 7, 0.0, fyp) if t == 1 else fyp)
                put(4, jnp.where(block_first, 0.0, fzm))
                put(5, jnp.where(block_last, 0.0, fzp))
                put(6, d)
                spread = jnp.where(block_last, fzp, pltpu.roll(fzp, 1, 1))
                near = jnp.logical_or(block_last, block_first)
                spread = jnp.where(near, spread, pltpu.roll(spread, 2, 1))
                near = jnp.logical_or(block_last, place <= 2)
                spread = jnp.where(near, spread, pltpu.roll(spread, 4, 1))
                near = jnp.logical_or(block_last, place <= 6)
                spread = jnp.where(near, spread, pltpu.roll(spread, 8, 1))
                put(7, spread)
                put(8, fyp)
                WX[pl.ds(8 * t, 8), :] = fxp

    def first(l):
        base = pl.multiple_of(l * ROWS, 8) + 8
        for t in range(4):
            inv = W[l, 6, pl.ds(8 * t, 8), :]
            for c in range(NF):
                r = c * NY + 8 * t
                B0[pl.ds(base + r, 8), :] = S[l, pl.ds(r, 8), :] * inv

    def sweep(old, new, l):
        base = pl.multiple_of(l * ROWS, 8) + 8
        for t in range(4):
            wxm, wxp, wym, wyp, wzm, wzp = [W[l, q, pl.ds(8 * t, 8), :] for q in range(6)]
            for c in range(NF):
                r = base + c * NY + 8 * t
                mid = old[pl.ds(r, 8), :]
                x_part = wxm * old[pl.ds(r - ROWS, 8), :] + wxp * old[pl.ds(r + ROWS, 8), :]
                y_part = wym * old[pl.ds(r - 1, 8), :] + wyp * old[pl.ds(r + 1, 8), :]
                z_part = wzm * pltpu.roll(mid, 1, 1) + wzp * pltpu.roll(mid, NZ - 1, 1)
                new[pl.ds(r, 8), :] = (B0[pl.ds(r, 8), :] + x_part) + (y_part + z_part)

    def many(body, start, step, count):
        def run(i, carry):
            body(start + i * step)
            return carry

        lax.fori_loop(0, count, run, 0)

    pairs = [(c, e) for c in range(NF) for e in range(c, NF)]
    near1 = jnp.logical_or(block_last, block_first)
    near2 = jnp.logical_or(block_last, place <= 2)
    near3 = jnp.logical_or(block_last, place <= 6)

    def couple(start, step, count):
        for yb in range(2):
            def run(i, accs):
                l = start + i * step
                x = l - LO
                base = pl.multiple_of(l * ROWS, 8) + 8
                ubase = pl.multiple_of(x * (NU * NY), 8)
                accs = list(accs)
                for tt in range(2):
                    t = 2 * yb + tt
                    u = [U[pl.ds(ubase + q * NY + 8 * t, 8), :] for q in range(7)]
                    bs = [B3[pl.ds(base + c * NY + 8 * t, 8), :] for c in range(NF)]
                    for e in range(NF):
                        r = base + e * NY + 8 * t
                        total = u[6] * bs[e]
                        total -= u[0] * B3[pl.ds(r - ROWS, 8), :] + u[1] * B3[pl.ds(r + ROWS, 8), :]
                        total -= u[2] * B3[pl.ds(r - 1, 8), :] + u[3] * B3[pl.ds(r + 1, 8), :]
                        total -= u[4] * pltpu.roll(bs[e], 1, 1) + u[5] * pltpu.roll(bs[e], NZ - 1, 1)
                        for p, (c, e2) in enumerate(pairs):
                            if e2 == e:
                                accs[p] = accs[p] + bs[c] * total
                    m = [jnp.where(near1, bs[2 * q], pltpu.roll(bs[2 * q + 1], 2, 1)) for q in range(4)]
                    m = [jnp.where(near2, m[2 * q], pltpu.roll(m[2 * q + 1], 4, 1)) for q in range(2)]
                    v = jnp.where(near3, m[0], pltpu.roll(m[1], 8, 1))
                    vr = pl.ds(pl.multiple_of(yb * 256 + x * 16, 8) + 8 * tt, 8)
                    VV[vr, :] = v
                    VW[vr, :] = v * U[pl.ds(ubase + 7 * NY + 8 * t, 8), :]
                return tuple(accs)

            accs = tuple(ACC[yb, p] for p in range(len(pairs)))
            accs = lax.fori_loop(0, count, run, accs)
            for p in range(len(pairs)):
                ACC[yb, p] = accs[p]

    def prep_first(l):
        prep(l, True)
        first(l)

    def prep_two(l):
        prep(l, True)
        prep(l + 1, True)

    many(prep_two, LO + 1, 2, NXL // 2 - 1)
    many(first, LO + 1, 1, NXL - 2)
    many(functools.partial(sweep, B0, B1), LO + 2, 1, NXL - 4)
    many(functools.partial(sweep, B1, B2), LO + 3, 1, NXL - 6)
    many(functools.partial(sweep, B2, B3), LO + 4, 1, NXL - 8)
    couple(LO + 5, 1, NXL - 10)

    @pl.when(has_low)
    def _():
        up_perm().wait_recv()

    @pl.when(has_high)
    def _():
        down_perm().wait_recv()

    many(prep_first, LO, NXL - 1, 2)
    many(lambda l: prep(l, False), 0, 1, LO)
    many(lambda l: prep(l, False), LO + NXL, 1, HI)

    def stage(k, carry):
        @pl.when(jnp.logical_and(has_low, k > 0))
        def _():
            up_layer(k).wait_recv()

        @pl.when(jnp.logical_and(has_high, k > 0))
        def _():
            down_layer(k).wait_recv()

        @pl.when(k > 0)
        def _():
            many(first, LO - k, NXL - 1 + 2 * k, 2)

        many(functools.partial(sweep, B0, B1), LO + 1 - k, NXL - 3 + 2 * k, 2)
        many(functools.partial(sweep, B1, B2), LO + 2 - k, NXL - 5 + 2 * k, 2)
        many(functools.partial(sweep, B2, B3), LO + 3 - k, NXL - 7 + 2 * k, 2)
        couple(LO + 4 - k, NXL - 9 + 2 * k, 2)
        return carry

    lax.fori_loop(0, LO + 1, stage, 0)
    couple(LO, NXL - 1, 2)

    for h in range(2):
        def rows(ref, first_row, stride):
            return ref[pl.ds(first_row, 8, stride=stride), :]

        wy = rows(U, (8 * h * NU + 8) * NY + B - 1, NU * NY)
        left = [wy * rows(B3, (LO + 8 * h) * ROWS + 8 + c * NY + B - 1, ROWS) for c in range(NF)]
        right = [rows(B3, (LO + 8 * h) * ROWS + 8 + e * NY + B, ROWS) for e in range(NF)]
        for c in range(NF):
            for e in range(NF):
                value = left[c] * right[e]
                if h == 0:
                    CY[pl.ds((c * NF + e) * 8, 8), :] = value
                else:
                    CY[pl.ds((c * NF + e) * 8, 8), :] += value

    @pl.when(has_high)
    def _():
        down_layer(HI).wait_recv()

    first(LO + NXL + 3)
    sweep(B0, B1, LO + NXL + 2)
    sweep(B1, B2, LO + NXL + 1)
    sweep(B2, B3, LO + NXL)

    base = (LO + NXL - 1) * ROWS + 8
    for yb in range(2):
        def pick(layer, c, tt):
            row = c * NY if isinstance(c, int) else pl.multiple_of(c * NY, 8)
            return B3[pl.ds(row + base + layer * ROWS + 16 * yb + 8 * tt, 8), :]

        def cross(c, carry):
            left = [WX[pl.ds(16 * yb + 8 * tt, 8), :] * pick(0, c, tt) for tt in range(2)]
            for e in range(NF):
                row = pl.multiple_of(c * (NF * 16), 8) + (e * 2 + yb) * 8
                CX[pl.ds(row, 8), :] = left[0] * pick(1, e, 0) + left[1] * pick(1, e, 1)
            return carry

        lax.fori_loop(0, NF, cross, 0)

    def fold(ref, count):
        def run(q, carry):
            row = pl.multiple_of(q * 64, 8)
            parts = [ref[pl.ds(row + k, 8, stride=8), :] for k in range(8)]
            parts = [parts[k] + parts[k + 4] for k in range(4)]
            TOT[pl.ds(pl.multiple_of(q * 8, 8), 8), :] = (parts[0] + parts[1]) + (parts[2] + parts[3])
            return carry

        lax.fori_loop(0, count, run, 0)
        return TOT[pl.ds(0, 8 * count), :]

    zi = lax.broadcasted_iota(jnp.int32, (NZ, NZ), 0)
    zj = lax.broadcasted_iota(jnp.int32, (NZ, NZ), 1)
    group = (zi // B == zj).astype(F32)

    for yb in range(2):
        for p, (c, e) in enumerate(pairs):
            value = ACC[yb, p]
            RED[pl.ds(((c * NF + e) * 2 + yb) * 8, 8), :] = value
            if c != e:
                RED[pl.ds(((e * NF + c) * 2 + yb) * 8, 8), :] = value

    def dot(a, b):
        return lax.dot_general(a, b, (((1,), (0,)), ((), ())), precision=HIGH, preferred_element_type=F32)

    blk = fold(RED, 16)
    blk_out[...] = dot(blk, group)[:, :8] * (1.0 / B**3)
    fx = fold(CX, 16)
    face_out[pl.ds(0, 128), :] = dot(fx, group)[:, :8] * (-1.0 / B**2)

    fy = fold(CY, 8)
    fy = dot(fy, group) * (-1.0 / B**2)
    zeros64 = jnp.zeros((64, NZ), F32)
    RED[pl.ds(0, 64, stride=2), :] = fy
    RED[pl.ds(1, 64, stride=2), :] = zeros64

    def slot(z):
        s = lax.rem(z - (B - 1) + NZ, NZ)
        return s // B, (s % B) // 2, s % 2

    ij, ic, ip = slot(zi)
    jj, je, jp = slot(zj)
    keep = jnp.logical_and(jnp.logical_and(ij == jj, ij < NZ // B - 1), jnp.logical_and(ip == 0, jp == 1))
    spread = jnp.logical_and(ip == 1, zj == ic * 8 + ij).astype(F32)
    wide = lax.broadcasted_iota(jnp.int32, (8, NZ), 1)
    wj, wc, wp = slot(wide)
    gather = jnp.logical_and(wp == 0, wc == lax.broadcasted_iota(jnp.int32, (8, NZ), 0)).astype(F32)
    for yb in range(2):
        gram = lax.dot_general(VV[pl.ds(yb * 256, 256), :], VW[pl.ds(yb * 256, 256), :],
                               (((0,), (0,)), ((), ())), precision=HIGH, preferred_element_type=F32)
        gram = jnp.where(keep, gram, 0.0)
        out = dot(gather, dot(gram, spread)) * (-1.0 / B**2)
        for e in range(NF):
            value = out if e == 0 else pltpu.roll(out, NZ - 8 * e, 1)
            RED[pl.ds(128 + e * 2 + yb, 8, stride=16), :] = value
    face_out[pl.ds(128, 256), :] = RED[pl.ds(0, 256), :][:, :8]

    @pl.when(has_low)
    def _():
        down_perm().wait_send()
        for k in range(1, HI + 1):
            down_layer(k).wait_send()

    @pl.when(has_high)
    def _():
        up_perm().wait_send()
        for k in range(1, LO + 1):
            up_layer(k).wait_send()


def on_device(n, permeability, sources):
    blk, face = pl.pallas_call(
        functools.partial(kernel, n),
        out_shape=(jax.ShapeDtypeStruct((NF * NF * 2, 8), F32),
                   jax.ShapeDtypeStruct((3 * NF * NF * 2, 8), F32)),
        in_specs=[pl.BlockSpec(memory_space=pl.ANY)] * 2,
        out_specs=(pl.BlockSpec(memory_space=pltpu.VMEM),) * 2,
        scratch_shapes=[
            pltpu.VMEM((LAYERS + 2, NY + 16, NZ), F32),
            pltpu.VMEM((LAYERS, NF * NY, NZ), F32),
            pltpu.VMEM((LAYERS * ROWS, NZ), F32),
            pltpu.VMEM((LAYERS * ROWS, NZ), F32),
            pltpu.VMEM((LAYERS * ROWS, NZ), F32),
            pltpu.VMEM((LAYERS * ROWS, NZ), F32),
            pltpu.VMEM((LAYERS, 7, NY, NZ), F32),
            pltpu.VMEM((NXL * NU * NY, NZ), F32),
            pltpu.VMEM((NY, NZ), F32),
            pltpu.VMEM((2, 36, 8, NZ), F32),
            pltpu.VMEM((NF * NF * 2 * 8, NZ), F32),
            pltpu.VMEM((NF * NF * 8, NZ), F32),
            pltpu.VMEM((512, NZ), F32),
            pltpu.VMEM((512, NZ), F32),
            pltpu.VMEM((NF * NF * 2 * 8, NZ), F32),
            pltpu.VMEM((NF * NF * 2, NZ), F32),
            pltpu.SemaphoreType.DMA((NF + 1,)),
            pltpu.SemaphoreType.DMA((2, HI + 1)),
            pltpu.SemaphoreType.DMA((2, HI + 1)),
        ],
        compiler_params=pltpu.CompilerParams(
            collective_id=0, has_side_effects=True, vmem_limit_bytes=40 * 1024 * 1024),
    )(permeability, sources)
    return blk.reshape(NF, NF, 1, 2, 8), face.reshape(3, NF, NF, 1, 2, 8)


def solution(mesh):
    return jax.shard_map(
        functools.partial(on_device, mesh.shape["gx"]),
        mesh=mesh,
        in_specs=(P("gx", "grp", None), P(None, "gx", "grp", None)),
        out_specs=(P(None, None, "gx", "grp", None), P(None, None, None, "gx", "grp", None)),
        check_vma=False,
    )
```

```python
import functools

import jax
import jax.numpy as jnp
from jax import lax
from jax.experimental import pallas as pl
from jax.experimental.pallas import tpu as pltpu
from jax.sharding import PartitionSpec as P

B = 16
WEIGHT_Z = 0.1
NF = 8
NXL = 16
NY = 32
NZ = 128
LO = 3
HI = 4
LAYERS = LO + NXL + HI
ROWS = 8 + NF * NY + 8
NU = 9
F32 = jnp.float32
HIGH = lax.Precision.HIGHEST
MESH = pl.DeviceIdType.MESH


def kernel(n, perm, src, blk_out, face_out,
           K, S, B0, B1, B2, B3, W, U, WX, ACC, CX, CY, VV, VW, RED, TOT,
           load_sem, send_sem, recv_sem):
    me = lax.axis_index("gx")
    has_low = me > 0
    has_high = me < n - 1

    barrier = pltpu.get_barrier_semaphore()

    @pl.when(has_low)
    def _():
        pl.semaphore_signal(barrier, inc=1, device_id={"gx": me - 1}, device_id_type=MESH)

    @pl.when(has_high)
    def _():
        pl.semaphore_signal(barrier, inc=1, device_id={"gx": me + 1}, device_id_type=MESH)

    loads = [pltpu.make_async_copy(perm, K.at[pl.ds(LO + 1, NXL), pl.ds(8, NY)], load_sem.at[NF])]
    for c in range(NF):
        loads.append(pltpu.make_async_copy(
            src.at[c], S.at[pl.ds(LO, NXL), pl.ds(c * NY, NY)], load_sem.at[c]))
    for copy in loads:
        copy.start()

    zero8 = jnp.zeros((8, NZ), F32)

    def pads(l, carry):
        K[l, pl.ds(0, 8), :] = zero8
        K[l, pl.ds(8 + NY, 8), :] = zero8
        return carry

    lax.fori_loop(0, LAYERS + 2, pads, 0)

    def pads_b(l, carry):
        base = pl.multiple_of(l * ROWS, 8)
        for ref in (B0, B1, B2, B3):
            ref[pl.ds(base, 8), :] = zero8
            ref[pl.ds(base + ROWS - 8, 8), :] = zero8
        return carry

    lax.fori_loop(0, LAYERS, pads_b, 0)
    for l in (LO - 1, LO + NXL):
        B3[pl.ds(l * ROWS, ROWS), :] = jnp.zeros((ROWS, NZ), F32)
    ACC[...] = jnp.zeros_like(ACC)

    @pl.when(me == 0)
    def _():
        K[pl.ds(0, LO + 1), pl.ds(8, NY), :] = jnp.zeros((LO + 1, NY, NZ), F32)

        def clear(l, carry):
            S[l] = jnp.zeros((NF * NY, NZ), F32)
            return carry

        lax.fori_loop(0, LO, clear, 0)

    @pl.when(me == n - 1)
    def _():
        K[pl.ds(LO + NXL + 1, HI + 1), pl.ds(8, NY), :] = jnp.zeros((HI + 1, NY, NZ), F32)

        def clear(l, carry):
            S[l] = jnp.zeros((NF * NY, NZ), F32)
            return carry

        lax.fori_loop(LO + NXL, LAYERS, clear, 0)

    def up_perm():
        return pltpu.make_async_remote_copy(
            src_ref=K.at[pl.ds(NXL, LO + 1), pl.ds(8, NY)],
            dst_ref=K.at[pl.ds(0, LO + 1), pl.ds(8, NY)],
            send_sem=send_sem.at[0, 0], recv_sem=recv_sem.at[0, 0],
            device_id={"gx": me + 1}, device_id_type=MESH)

    def down_perm():
        return pltpu.make_async_remote_copy(
            src_ref=K.at[pl.ds(LO + 1, HI + 1), pl.ds(8, NY)],
            dst_ref=K.at[pl.ds(LO + NXL + 1, HI + 1), pl.ds(8, NY)],
            send_sem=send_sem.at[1, 0], recv_sem=recv_sem.at[1, 0],
            device_id={"gx": me - 1}, device_id_type=MESH)

    def up_layer(k):
        return pltpu.make_async_remote_copy(
            src_ref=S.at[LO + NXL - k], dst_ref=S.at[LO - k],
            send_sem=send_sem.at[0, k], recv_sem=recv_sem.at[0, k],
            device_id={"gx": me + 1}, device_id_type=MESH)

    def down_layer(k):
        return pltpu.make_async_remote_copy(
            src_ref=S.at[LO - 1 + k], dst_ref=S.at[LO + NXL - 1 + k],
            send_sem=send_sem.at[1, k], recv_sem=recv_sem.at[1, k],
            device_id={"gx": me - 1}, device_id_type=MESH)

    pl.semaphore_wait(barrier, has_low.astype(jnp.int32) + has_high.astype(jnp.int32))

    loads[0].wait()

    @pl.when(has_low)
    def _():
        down_perm().start()

    @pl.when(has_high)
    def _():
        up_perm().start()

    for copy in loads[1:]:
        copy.wait()

    @pl.when(has_low)
    def _():
        for k in range(1, HI + 1):
            down_layer(k).start()

    @pl.when(has_high)
    def _():
        for k in range(1, LO + 1):
            up_layer(k).start()

    lane = lax.broadcasted_iota(jnp.int32, (8, NZ), 1)
    sub = lax.broadcasted_iota(jnp.int32, (8, NZ), 0)
    low_lane = lane == 0
    high_lane = lane == NZ - 1
    place = lane % B
    block_first = place == 0
    block_last = place == B - 1

    def prep(l, own):
        dead = jnp.logical_or(jnp.logical_and(l < LO, me == 0),
                              jnp.logical_and(l >= LO + NXL, me == n - 1))
        alive = jnp.where(dead, 0.0, 1.0).astype(F32)
        x = l - LO
        for t in range(4):
            k = K[l + 1, pl.ds(8 + 8 * t, 8), :]
            fxm = 0.5 * (k + K[l, pl.ds(8 + 8 * t, 8), :])
            fxp = 0.5 * (k + K[l + 2, pl.ds(8 + 8 * t, 8), :])
            fym = 0.5 * (k + K[l + 1, pl.ds(7 + 8 * t, 8), :])
            fyp = 0.5 * (k + K[l + 1, pl.ds(9 + 8 * t, 8), :])
            fzm = (0.5 * WEIGHT_Z) * (k + jnp.where(low_lane, 0.0, pltpu.roll(k, 1, 1)))
            fzp = (0.5 * WEIGHT_Z) * (k + jnp.where(high_lane, 0.0, pltpu.roll(k, NZ - 1, 1)))
            d = fxm + fxp + fym + fyp + fzm + fzp
            inv = jnp.where(alive > 0.5, 1.0 / d, 0.0)
            if t == 0:
                fym = jnp.where(sub == 0, 0.0, fym)
            if t == 3:
                fyp = jnp.where(sub == 7, 0.0, fyp)
            fzm = jnp.where(low_lane, 0.0, fzm)
            fzp = jnp.where(high_lane, 0.0, fzp)
            for q, f in enumerate((fxm, fxp, fym, fyp, fzm, fzp)):
                W[l, q, pl.ds(8 * t, 8), :] = f * inv
            W[l, 6, pl.ds(8 * t, 8), :] = inv
            if own:
                inner_m = jnp.where(x == 0, 0.0, 1.0).astype(F32)
                inner_p = jnp.where(x == NXL - 1, 0.0, 1.0).astype(F32)
                base = pl.multiple_of(x * (NU * NY), 8) + 8 * t

                def put(q, f):
                    U[pl.ds(base + q * NY, 8), :] = f

                put(0, fxm * inner_m)
                put(1, fxp * inner_p)
                put(2, jnp.where(sub == 0, 0.0, fym) if t == 2 else fym)
                put(3, jnp.where(sub == 7, 0.0, fyp) if t == 1 else fyp)
                put(4, jnp.where(block_first, 0.0, fzm))
                put(5, jnp.where(block_last, 0.0, fzp))
                put(6, d)
                spread = jnp.where(block_last, fzp, pltpu.roll(fzp, 1, 1))
                near = jnp.logical_or(block_last, block_first)
                spread = jnp.where(near, spread, pltpu.roll(spread, 2, 1))
                near = jnp.logical_or(block_last, place <= 2)
                spread = jnp.where(near, spread, pltpu.roll(spread, 4, 1))
                near = jnp.logical_or(block_last, place <= 6)
                spread = jnp.where(near, spread, pltpu.roll(spread, 8, 1))
                put(7, spread)
                put(8, fyp)
                WX[pl.ds(8 * t, 8), :] = fxp

    def first(l):
        base = pl.multiple_of(l * ROWS, 8) + 8
        for t in range(4):
            inv = W[l, 6, pl.ds(8 * t, 8), :]
            for c in range(NF):
                r = c * NY + 8 * t
                B0[pl.ds(base + r, 8), :] = S[l, pl.ds(r, 8), :] * inv

    def sweep(old, new, l):
        base = pl.multiple_of(l * ROWS, 8) + 8
        for t in range(4):
            wxm, wxp, wym, wyp, wzm, wzp = [W[l, q, pl.ds(8 * t, 8), :] for q in range(6)]
            for c in range(NF):
                r = base + c * NY + 8 * t
                mid = old[pl.ds(r, 8), :]
                x_part = wxm * old[pl.ds(r - ROWS, 8), :] + wxp * old[pl.ds(r + ROWS, 8), :]
                y_part = wym * old[pl.ds(r - 1, 8), :] + wyp * old[pl.ds(r + 1, 8), :]
                z_part = wzm * pltpu.roll(mid, 1, 1) + wzp * pltpu.roll(mid, NZ - 1, 1)
                new[pl.ds(r, 8), :] = (B0[pl.ds(r, 8), :] + x_part) + (y_part + z_part)

    def many(body, start, step, count):
        def run(i, carry):
            body(start + 2 * i * step)
            body(start + (2 * i + 1) * step)
            return carry

        if count == 2:
            run(0, 0)
        else:
            lax.fori_loop(0, count // 2, run, 0)
        if count % 2:
            body(start + (count - 1) * step)

    pairs = [(c, e) for c in range(NF) for e in range(c, NF)]
    near1 = jnp.logical_or(block_last, block_first)
    near2 = jnp.logical_or(block_last, place <= 2)
    near3 = jnp.logical_or(block_last, place <= 6)

    def couple(start, step, count):
        for yb in range(2):
            def run(i, accs):
                l = start + i * step
                x = l - LO
                base = pl.multiple_of(l * ROWS, 8) + 8
                ubase = pl.multiple_of(x * (NU * NY), 8)
                accs = list(accs)
                for tt in range(2):
                    t = 2 * yb + tt
                    u = [U[pl.ds(ubase + q * NY + 8 * t, 8), :] for q in range(7)]
                    bs = [B3[pl.ds(base + c * NY + 8 * t, 8), :] for c in range(NF)]
                    for e in range(NF):
                        r = base + e * NY + 8 * t
                        total = u[6] * bs[e]
                        total -= u[0] * B3[pl.ds(r - ROWS, 8), :] + u[1] * B3[pl.ds(r + ROWS, 8), :]
                        total -= u[2] * B3[pl.ds(r - 1, 8), :] + u[3] * B3[pl.ds(r + 1, 8), :]
                        total -= u[4] * pltpu.roll(bs[e], 1, 1) + u[5] * pltpu.roll(bs[e], NZ - 1, 1)
                        for p, (c, e2) in enumerate(pairs):
                            if e2 == e:
                                accs[p] = accs[p] + bs[c] * total
                    m = [jnp.where(near1, bs[2 * q], pltpu.roll(bs[2 * q + 1], 2, 1)) for q in range(4)]
                    m = [jnp.where(near2, m[2 * q], pltpu.roll(m[2 * q + 1], 4, 1)) for q in range(2)]
                    v = jnp.where(near3, m[0], pltpu.roll(m[1], 8, 1))
                    vr = pl.ds(pl.multiple_of(yb * 256 + x * 16, 8) + 8 * tt, 8)
                    VV[vr, :] = v
                    VW[vr, :] = v * U[pl.ds(ubase + 7 * NY + 8 * t, 8), :]
                return tuple(accs)

            accs = tuple(ACC[yb, p] for p in range(len(pairs)))
            accs = lax.fori_loop(0, count, run, accs)
            for p in range(len(pairs)):
                ACC[yb, p] = accs[p]

    def prep_first(l):
        prep(l, True)
        first(l)

    many(lambda l: prep(l, True), LO + 1, 1, NXL - 2)
    many(first, LO + 1, 1, NXL - 2)
    many(functools.partial(sweep, B0, B1), LO + 2, 1, NXL - 4)
    many(functools.partial(sweep, B1, B2), LO + 3, 1, NXL - 6)
    many(functools.partial(sweep, B2, B3), LO + 4, 1, NXL - 8)
    couple(LO + 5, 1, NXL - 10)

    @pl.when(has_low)
    def _():
        up_perm().wait_recv()

    @pl.when(has_high)
    def _():
        down_perm().wait_recv()

    many(prep_first, LO, NXL - 1, 2)
    many(lambda l: prep(l, False), 0, 1, LO)
    many(lambda l: prep(l, False), LO + NXL, 1, HI)

    def stage(k, carry):
        @pl.when(jnp.logical_and(has_low, k > 0))
        def _():
            up_layer(k).wait_recv()

        @pl.when(jnp.logical_and(has_high, k > 0))
        def _():
            down_layer(k).wait_recv()

        @pl.when(k > 0)
        def _():
            many(first, LO - k, NXL - 1 + 2 * k, 2)

        many(functools.partial(sweep, B0, B1), LO + 1 - k, NXL - 3 + 2 * k, 2)
        many(functools.partial(sweep, B1, B2), LO + 2 - k, NXL - 5 + 2 * k, 2)
        many(functools.partial(sweep, B2, B3), LO + 3 - k, NXL - 7 + 2 * k, 2)
        couple(LO + 4 - k, NXL - 9 + 2 * k, 2)
        return carry

    lax.fori_loop(0, LO + 1, stage, 0)
    couple(LO, NXL - 1, 2)

    for h in range(2):
        def rows(ref, first_row, stride):
            return ref[pl.ds(first_row, 8, stride=stride), :]

        wy = rows(U, (8 * h * NU + 8) * NY + B - 1, NU * NY)
        left = [wy * rows(B3, (LO + 8 * h) * ROWS + 8 + c * NY + B - 1, ROWS) for c in range(NF)]
        right = [rows(B3, (LO + 8 * h) * ROWS + 8 + e * NY + B, ROWS) for e in range(NF)]
        for c in range(NF):
            for e in range(NF):
                value = left[c] * right[e]
                if h == 0:
                    CY[pl.ds((c * NF + e) * 8, 8), :] = value
                else:
                    CY[pl.ds((c * NF + e) * 8, 8), :] += value

    @pl.when(has_high)
    def _():
        down_layer(HI).wait_recv()

    first(LO + NXL + 3)
    sweep(B0, B1, LO + NXL + 2)
    sweep(B1, B2, LO + NXL + 1)
    sweep(B2, B3, LO + NXL)

    base = (LO + NXL - 1) * ROWS + 8
    for yb in range(2):
        def pick(layer, c, tt):
            row = c * NY if isinstance(c, int) else pl.multiple_of(c * NY, 8)
            return B3[pl.ds(row + base + layer * ROWS + 16 * yb + 8 * tt, 8), :]

        def cross(c, carry):
            left = [WX[pl.ds(16 * yb + 8 * tt, 8), :] * pick(0, c, tt) for tt in range(2)]
            for e in range(NF):
                row = pl.multiple_of(c * (NF * 16), 8) + (e * 2 + yb) * 8
                CX[pl.ds(row, 8), :] = left[0] * pick(1, e, 0) + left[1] * pick(1, e, 1)
            return carry

        lax.fori_loop(0, NF, cross, 0)

    def fold(ref, count):
        def run(q, carry):
            row = pl.multiple_of(q * 64, 8)
            parts = [ref[pl.ds(row + k, 8, stride=8), :] for k in range(8)]
            parts = [parts[k] + parts[k + 4] for k in range(4)]
            TOT[pl.ds(pl.multiple_of(q * 8, 8), 8), :] = (parts[0] + parts[1]) + (parts[2] + parts[3])
            return carry

        lax.fori_loop(0, count, run, 0)
        return TOT[pl.ds(0, 8 * count), :]

    zi = lax.broadcasted_iota(jnp.int32, (NZ, NZ), 0)
    zj = lax.broadcasted_iota(jnp.int32, (NZ, NZ), 1)
    group = (zi // B == zj).astype(F32)

    for yb in range(2):
        for p, (c, e) in enumerate(pairs):
            value = ACC[yb, p]
            RED[pl.ds(((c * NF + e) * 2 + yb) * 8, 8), :] = value
            if c != e:
                RED[pl.ds(((e * NF + c) * 2 + yb) * 8, 8), :] = value

    def dot(a, b):
        return lax.dot_general(a, b, (((1,), (0,)), ((), ())), precision=HIGH, preferred_element_type=F32)

    blk = fold(RED, 16)
    blk_out[...] = dot(blk, group)[:, :8] * (1.0 / B**3)
    fx = fold(CX, 16)
    face_out[pl.ds(0, 128), :] = dot(fx, group)[:, :8] * (-1.0 / B**2)

    fy = fold(CY, 8)
    fy = dot(fy, group) * (-1.0 / B**2)
    zeros64 = jnp.zeros((64, NZ), F32)
    RED[pl.ds(0, 64, stride=2), :] = fy
    RED[pl.ds(1, 64, stride=2), :] = zeros64

    def slot(z):
        s = lax.rem(z - (B - 1) + NZ, NZ)
        return s // B, (s % B) // 2, s % 2

    ij, ic, ip = slot(zi)
    jj, je, jp = slot(zj)
    keep = jnp.logical_and(jnp.logical_and(ij == jj, ij < NZ // B - 1), jnp.logical_and(ip == 0, jp == 1))
    spread = jnp.logical_and(ip == 1, zj == ic * 8 + ij).astype(F32)
    wide = lax.broadcasted_iota(jnp.int32, (8, NZ), 1)
    wj, wc, wp = slot(wide)
    gather = jnp.logical_and(wp == 0, wc == lax.broadcasted_iota(jnp.int32, (8, NZ), 0)).astype(F32)
    for yb in range(2):
        gram = lax.dot_general(VV[pl.ds(yb * 256, 256), :], VW[pl.ds(yb * 256, 256), :],
                               (((0,), (0,)), ((), ())), precision=HIGH, preferred_element_type=F32)
        gram = jnp.where(keep, gram, 0.0)
        out = dot(gather, dot(gram, spread)) * (-1.0 / B**2)
        for e in range(NF):
            value = out if e == 0 else pltpu.roll(out, NZ - 8 * e, 1)
            RED[pl.ds(128 + e * 2 + yb, 8, stride=16), :] = value
    face_out[pl.ds(128, 256), :] = RED[pl.ds(0, 256), :][:, :8]

    @pl.when(has_low)
    def _():
        down_perm().wait_send()
        for k in range(1, HI + 1):
            down_layer(k).wait_send()

    @pl.when(has_high)
    def _():
        up_perm().wait_send()
        for k in range(1, LO + 1):
            up_layer(k).wait_send()


def on_device(n, permeability, sources):
    blk, face = pl.pallas_call(
        functools.partial(kernel, n),
        out_shape=(jax.ShapeDtypeStruct((NF * NF * 2, 8), F32),
                   jax.ShapeDtypeStruct((3 * NF * NF * 2, 8), F32)),
        in_specs=[pl.BlockSpec(memory_space=pl.ANY)] * 2,
        out_specs=(pl.BlockSpec(memory_space=pltpu.VMEM),) * 2,
        scratch_shapes=[
            pltpu.VMEM((LAYERS + 2, NY + 16, NZ), F32),
            pltpu.VMEM((LAYERS, NF * NY, NZ), F32),
            pltpu.VMEM((LAYERS * ROWS, NZ), F32),
            pltpu.VMEM((LAYERS * ROWS, NZ), F32),
            pltpu.VMEM((LAYERS * ROWS, NZ), F32),
            pltpu.VMEM((LAYERS * ROWS, NZ), F32),
            pltpu.VMEM((LAYERS, 7, NY, NZ), F32),
            pltpu.VMEM((NXL * NU * NY, NZ), F32),
            pltpu.VMEM((NY, NZ), F32),
            pltpu.VMEM((2, 36, 8, NZ), F32),
            pltpu.VMEM((NF * NF * 2 * 8, NZ), F32),
            pltpu.VMEM((NF * NF * 8, NZ), F32),
            pltpu.VMEM((512, NZ), F32),
            pltpu.VMEM((512, NZ), F32),
            pltpu.VMEM((NF * NF * 2 * 8, NZ), F32),
            pltpu.VMEM((NF * NF * 2, NZ), F32),
            pltpu.SemaphoreType.DMA((NF + 1,)),
            pltpu.SemaphoreType.DMA((2, HI + 1)),
            pltpu.SemaphoreType.DMA((2, HI + 1)),
        ],
        compiler_params=pltpu.CompilerParams(
            collective_id=0, has_side_effects=True, vmem_limit_bytes=40 * 1024 * 1024),
    )(permeability, sources)
    return blk.reshape(NF, NF, 1, 2, 8), face.reshape(3, NF, NF, 1, 2, 8)


def solution(mesh):
    return jax.shard_map(
        functools.partial(on_device, mesh.shape["gx"]),
        mesh=mesh,
        in_specs=(P("gx", "grp", None), P(None, "gx", "grp", None)),
        out_specs=(P(None, None, "gx", "grp", None), P(None, None, None, "gx", "grp", None)),
        check_vma=False,
    )
```
